32 devices in a mesh: pole: 2 (over core), sep: 16 (over z, y, x).
Axes of the slice: x: 2, y: 2, z: 4, core: 2. Of those that a mesh axis runs over, the one named last changes fastest.
Arguments:
- diag_inverse: bfloat16 [2, 128, 2, 256, 256], P('pole', 'sep'), may hold values from -6 to 6
- coupling: bfloat16 [2, 128, 2, 256, 256], P('pole', 'sep'), may hold values from -0.25 to 0.25
- ancestor_inverse: bfloat16 [2, 16, 2, 256, 256], P('pole', 'sep'), may hold values from -6 to 6
- pole_weight: float32 [2, 2], P('pole'), may hold values from -1 to 1
- ancestor_bit: int32 [128], P('sep'), may hold values from 0 to 3
- tile_blocks: int32 [16, 6], P('sep'), may hold values from 0 to 127, as said below
- tile_count: int32 [16], P('sep'), may hold values from 1 to 6
- orbital_values: bfloat16 [16, 6, 512, 256], P('sep', None, 'pole'), may hold values from -0.375 to 0.375
Outputs:
- density_grid: float32 [16, 512], P('sep', 'pole')
The draws below stay inside these ranges and needn't reach their ends.
Inputs may be any that keep to these rules, and one draw needn't show every extreme that they name: `tile_blocks`: entry (t, s) names a block owned by device t - 1, t or t + 1 of sep, block b being owned by device b // 8.
All inputs are finite; a program needn't handle non-finite values.
Results may differ from the reference program's by a relative error of at most 0.0035.
Values may be sent and summed in bfloat16 or wider, within the bound.
A program may use at most 64 MiB of HBM per device.

```python
import jax
import jax.numpy as jnp
from jax import lax

W = 256
B_DEV = 8
SLOTS = 6
LEVELS = 4
POLES = 2
NBLK = 128
NTILES = 16
PTS = 512
N_SEP = 16


def draw_tile_blocks(key, part):
    first, second = jax.random.split(jax.random.fold_in(key, 7))
    tile = jnp.arange(NTILES, dtype=jnp.int32)[:, None]
    offset = jax.random.randint(first, (NTILES, SLOTS), -1, 2, dtype=jnp.int32)
    device = jnp.clip(tile + offset, 0, NTILES - 1)
    local = jax.random.randint(second, (NTILES, SLOTS), 0, B_DEV, dtype=jnp.int32)
    return (device * B_DEV + local).astype(jnp.int32)


def touch_ends(array, stream_key, low, high):
    extent = array.shape
    spot = [jax.random.randint(jax.random.fold_in(stream_key, axis), (), 0, extent[axis]) for axis in range(len(extent))]
    array = array.at[tuple(spot)].set(low)
    longest = extent.index(max(extent))
    spot[longest] = (spot[longest] + 1) % extent[longest]
    return array.at[tuple(spot)].set(high)


def steps_of(key, extent, shards, low, high):
    level, own = 1.0, jax.random.fold_in(key, 6)
    for dim, shards_of in shards:
        heights = jnp.exp(jax.random.uniform(jax.random.fold_in(own, dim), (shards_of,), jnp.float32, low / len(shards), high / len(shards)))
        level = level * jnp.repeat(heights, extent[dim] // shards_of).reshape([-1 if axis == dim else 1 for axis in range(len(extent))])
    return level


def scatter_about(stream_key, dims, deviation, reach, pieces=(), kind=jnp.bfloat16):
    loudness = steps_of(stream_key, dims, pieces, -0.22, 0.18) if pieces else 1.0
    array = jax.random.normal(stream_key, dims, jnp.float32) * deviation * loudness
    return jnp.minimum(jnp.maximum(array, -reach), reach).astype(kind)


def setup_inputs(seed: int = 0) -> dict:
    streams_of = jax.random.split(jax.random.key(seed), 9)
    diag_inverse = scatter_about(streams_of[0], (POLES, NBLK, 2, W, W), 1.0, 6.0, ((0, 2), (1, 16)))
    coupling = scatter_about(streams_of[1], (POLES, NBLK, 2, W, W), (2 * W) ** -0.5, 0.25, ((0, 2), (1, 16)))
    ancestor_inverse = scatter_about(streams_of[2], (POLES, N_SEP, 2, W, W), 1.0, 6.0, ((0, 2), (1, 16)))
    pole_weight = jnp.clip(jax.random.uniform(streams_of[3], (POLES, 2), jnp.float32, -1.0, 1.0) * steps_of(streams_of[3], (POLES, 2), ((0, 2),), -0.4, 0.0), -1.0, 1.0)
    ancestor_bit = touch_ends(jax.random.randint(streams_of[4], (NBLK,), 0, LEVELS), jax.random.fold_in(streams_of[4], 1), 0, LEVELS - 1).astype(jnp.int32)
    tile_blocks = draw_tile_blocks(jax.random.fold_in(streams_of[8], 71), 0)
    tile_count = touch_ends(jax.random.randint(streams_of[6], (NTILES,), 1, SLOTS + 1), jax.random.fold_in(streams_of[6], 1), 1, SLOTS).astype(jnp.int32)
    orbital_values = scatter_about(streams_of[7], (NTILES, SLOTS, PTS, W), W ** -0.5, 0.375, ((0, 16), (2, 2)))
    return dict(diag_inverse=diag_inverse, coupling=coupling, ancestor_inverse=ancestor_inverse, pole_weight=pole_weight, ancestor_bit=ancestor_bit, tile_blocks=tile_blocks, tile_count=tile_count, orbital_values=orbital_values)


def product(left, right):
    return jnp.einsum("pij,pjk->pik", left, right, precision=lax.Precision.HIGHEST)


def product_t(left, right):
    return jnp.einsum("pij,pkj->pik", left, right, precision=lax.Precision.HIGHEST)


def reference(diag_inverse, coupling, ancestor_inverse, pole_weight, ancestor_bit, tile_blocks, tile_count, orbital_values):
    block_ids = jnp.arange(NBLK, dtype=jnp.int32)
    owner = jnp.bitwise_xor(block_ids // B_DEV, jnp.left_shift(jnp.ones_like(ancestor_bit), ancestor_bit)).astype(jnp.int32)

    def one_block(index):
        link = coupling[:, index].astype(jnp.float32)
        upper = ancestor_inverse[:, owner[index]].astype(jnp.float32)
        diag = diag_inverse[:, index].astype(jnp.float32)
        lr, li = link[:, 0], link[:, 1]
        gr, gi = upper[:, 0], upper[:, 1]
        mr = lax.optimization_barrier((product(lr, gr) - product(li, gi)).astype(jnp.bfloat16)).astype(jnp.float32)
        mi = lax.optimization_barrier((product(lr, gi) + product(li, gr)).astype(jnp.bfloat16)).astype(jnp.float32)
        green_real = diag[:, 0] + product_t(mr, lr) - product_t(mi, li)
        green_imag = diag[:, 1] + product_t(mr, li) + product_t(mi, lr)
        term = pole_weight[:, 0][:, None, None] * green_imag + pole_weight[:, 1][:, None, None] * green_real
        return jnp.sum(term, axis=0).astype(jnp.bfloat16)

    density = lax.map(one_block, block_ids)

    def one_tile(tile):
        blocks = jnp.take(density, tile_blocks[tile], axis=0).astype(jnp.float32)
        values = orbital_values[tile].astype(jnp.float32)
        inner = jnp.einsum("spw,swv->spv", values, blocks, precision=lax.Precision.HIGHEST)
        contribution = jnp.sum(values * inner, axis=-1)
        live = (jnp.arange(SLOTS, dtype=jnp.int32) < tile_count[tile])[:, None]
        return jnp.sum(jnp.where(live, contribution, jnp.float32(0.0)), axis=0)

    return lax.map(one_tile, jnp.arange(NTILES, dtype=jnp.int32))
```

```python
import functools

import jax
import jax.numpy as jnp
from jax import lax
from jax.experimental import pallas as pl
from jax.experimental.pallas import tpu as pltpu
from jax.sharding import PartitionSpec as P

LEVELS = 4
CHUNKS = 2
MESH = pl.DeviceIdType.MESH
F32 = jnp.float32
BF16 = jnp.bfloat16


def nt_dot(left, right):
    return lax.dot_general(left, right, (((1,), (1,)), ((), ())), preferred_element_type=F32)


def kernel(
    n_pole,
    n_sep,
    weight_ref,
    bit_ref,
    blocks_ref,
    count_ref,
    diag_hbm,
    link_hbm,
    upper_hbm,
    values_hbm,
    out_ref,
    diag,
    link,
    upper,
    values,
    packed,
    arrived,
    full,
    body,
    body_diag,
    part_send,
    part_recv,
    part_diag,
    mine,
    own,
    near,
    near_diag,
    chosen,
    list_send,
    list_recv,
    list_smem,
    local_sem,
    list_sem,
    upper_send_sem,
    upper_recv_sem,
    part_send_sem,
    part_recv_sem,
    pdiag_send_sem,
    pdiag_recv_sem,
    own_send_sem,
    own_recv_sem,
    halo_send_sem,
    halo_recv_sem,
    hdiag_send_sem,
    hdiag_recv_sem,
    fwd_send_sem,
    fwd_recv_sem,
    list_send_sem,
    list_recv_sem,
):
    pole = lax.axis_index("pole")
    me = lax.axis_index("sep")
    nblocks = link.shape[0]
    slots = values.shape[0]
    half = packed.shape[1]
    rows = mine.shape[1]
    per_chunk = nblocks // CHUNKS
    peers = range(1, n_pole)

    def peer(k):
        return lax.rem(pole + k, n_pole)

    def piece(q):
        return pl.ds(pl.multiple_of(q * rows, rows), rows)

    def partner(level):
        step = 2**level
        return me + step * (1 - 2 * lax.rem(me // step, 2))

    sides = ((0, me > 0, me - 1), (1, me < n_sep - 1, me + 1))

    def remote(src, dst, send, recv, where):
        return pltpu.make_async_remote_copy(
            src_ref=src, dst_ref=dst, send_sem=send, recv_sem=recv, device_id=where, device_id_type=MESH
        )

    loads = [
        pltpu.make_async_copy(src, dst, local_sem.at[i])
        for i, (src, dst) in enumerate(
            (
                (upper_hbm.at[0, 0], upper),
                (diag_hbm.at[0], diag),
                (link_hbm.at[0], link),
                (values_hbm.at[0], values),
            )
        )
    ]
    for load in loads:
        load.start()

    barrier = pltpu.get_barrier_semaphore()
    for k in peers:
        pl.semaphore_signal(barrier, inc=1, device_id={"pole": peer(k)}, device_id_type=MESH)
    for level in range(LEVELS):
        pl.semaphore_signal(barrier, inc=1, device_id={"sep": partner(level)}, device_id_type=MESH)
    for _, there, neighbour in sides:

        @pl.when(there)
        def _():
            pl.semaphore_signal(barrier, inc=1, device_id={"sep": neighbour}, device_id_type=MESH)

    row = lax.broadcasted_iota(jnp.int32, (half, half), 0)
    col = lax.broadcasted_iota(jnp.int32, (half, half), 1)
    above, below, on = row < col, row > col, row == col

    def diagonal(x):
        return jnp.sum(jnp.where(on, x, 0.0), axis=0, keepdims=True)

    wr, wi = weight_ref[0, 0], weight_ref[0, 1]

    lane = lax.broadcasted_iota(jnp.int32, list_send.shape, 1)
    listed = jnp.zeros(list_send.shape, jnp.int32)
    for s in range(slots):
        listed = jnp.where(lane == s, blocks_ref[0, s], listed)
    list_send[...] = listed

    loads[0].wait()
    doubled = []
    for part in range(2):
        g00 = upper[part, :half, :half].astype(F32)
        g01 = upper[part, :half, half:].astype(F32)
        g10 = upper[part, half:, :half].astype(F32)
        g11 = upper[part, half:, half:].astype(F32)
        doubled.append((g00 + g00.T, g01 + g10.T, g11 + g11.T))
    weighted = (
        [wr * a - wi * b for a, b in zip(*doubled)],
        [wr * b + wi * a for a, b in zip(*doubled)],
    )
    ends = []
    for part in range(2):
        s00, s01, s11 = weighted[part]
        packed[2 * part] = s01.astype(BF16)
        packed[2 * part + 1] = jnp.where(below, s11, s00).astype(BF16)
        ends.append(diagonal(s11))
    packed[4] = jnp.where(row == 0, ends[0], jnp.where(row == 1, ends[1], 0.0)).astype(BF16)

    pl.semaphore_wait(
        barrier, n_pole - 1 + LEVELS + (me > 0).astype(jnp.int32) + (me < n_sep - 1).astype(jnp.int32)
    )

    def upper_copies(level):
        where = {"sep": partner(level)}
        return (
            remote(
                packed.at[pl.ds(0, 4)],
                arrived.at[level, pl.ds(0, 4)],
                upper_send_sem.at[level, 0],
                upper_recv_sem.at[level, 0],
                where,
            ),
            remote(
                packed.at[4, pl.ds(0, 16)],
                arrived.at[level, 4, pl.ds(0, 16)],
                upper_send_sem.at[level, 1],
                upper_recv_sem.at[level, 1],
                where,
            ),
        )

    for level in reversed(range(LEVELS)):
        for copy in upper_copies(level):
            copy.start()

    def list_copy(d, neighbour, slot):
        return remote(
            list_send, list_recv.at[slot], list_send_sem.at[d], list_recv_sem.at[slot], {"sep": neighbour}
        )

    for d, there, neighbour in sides:

        @pl.when(there)
        def _():
            list_copy(d, neighbour, 1 - d).start()

    loads[1].wait()

    def fold(b, carry):
        def term(rows_at, cols_at):
            real = diag[b, 0, rows_at, cols_at].astype(F32)
            imag = diag[b, 1, rows_at, cols_at].astype(F32)
            return wr * imag + wi * real

        low, high = pl.ds(0, half), pl.ds(half, half)
        t00, t01, t10, t11 = term(low, low), term(low, high), term(high, low), term(high, high)
        body[b, :half, :] = t01 + t10.T
        body[b, half:, :] = jnp.where(above, t00 + t00.T, jnp.where(below, t11 + t11.T, t00))
        body_diag[pl.ds(b, 1), :] = diagonal(t11)
        return carry

    lax.fori_loop(0, nblocks, fold, 0)
    loads[2].wait()

    for d, there, neighbour in sides:

        @pl.when(there)
        def _():
            list_copy(d, neighbour, d).wait_recv()
            fetch = pltpu.make_async_copy(list_recv.at[d], list_smem.at[d], list_sem.at[d])
            fetch.start()
            fetch.wait()

    for level in range(LEVELS):
        for copy in upper_copies(level):
            copy.wait_recv()
        ends = arrived[level, 4, :16, :].astype(F32)
        symmetric = []
        for part in range(2):
            u01 = arrived[level, 2 * part]
            both = arrived[level, 2 * part + 1].astype(F32)
            turned = both.T
            g00 = jnp.where(below, turned, both)
            g11 = jnp.where(below, both, jnp.where(above, turned, ends[part : part + 1, :]))
            u10 = u01.astype(F32).T.astype(BF16)
            symmetric.append(((g00.astype(BF16), u01), (u10, g11.astype(BF16))))
        for i in range(2):
            for j in range(2):
                real, imag = symmetric[0][i][j], symmetric[1][i][j]
                r, c = i * half, j * half
                full[level, r : r + half, c : c + half] = real
                full[level, r : r + half, 2 * half + c : 3 * half + c] = imag
                full[level, 2 * half + r : 3 * half + r, c : c + half] = -imag
                full[level, 2 * half + r : 3 * half + r, 2 * half + c : 3 * half + c] = real

    def density(b, carry):
        real, imag = link[b, 0], link[b, 1]
        middle = jnp.dot(
            jnp.concatenate([real, imag], axis=1), full[bit_ref[b]], preferred_element_type=F32
        ).astype(BF16)
        crossed = jnp.concatenate([imag, real], axis=1)
        top = nt_dot(middle[:half], crossed)
        low = nt_dot(middle[half:], crossed[half:])
        corner = top[:, :half]
        body[b, :half, :] += top[:, half:]
        body[b, half:, :] += jnp.where(above, corner, jnp.where(below, low, 0.5 * corner))
        body_diag[pl.ds(b, 1), :] += 0.5 * diagonal(low)
        return carry

    def part_copy(chunk, k):
        at = pl.ds(chunk * per_chunk, per_chunk)
        return remote(
            part_send.at[k, at],
            part_recv.at[k, at],
            part_send_sem.at[chunk, k],
            part_recv_sem.at[chunk, k],
            {"pole": peer(k)},
        )

    def pdiag_copy(k):
        return remote(
            body_diag, part_diag.at[k], pdiag_send_sem.at[k], pdiag_recv_sem.at[k], {"pole": peer(k)}
        )

    for chunk in range(CHUNKS):
        lax.fori_loop(chunk * per_chunk, (chunk + 1) * per_chunk, density, 0)
        for k in peers:
            at = pl.ds(chunk * per_chunk, per_chunk)
            part_send[k, at] = body[at, piece(peer(k)), :]
            part_copy(chunk, k).start()
    for k in peers:
        pdiag_copy(k).start()

    for chunk in range(CHUNKS):
        at = pl.ds(chunk * per_chunk, per_chunk)
        total = body[at, piece(pole), :]
        for k in peers:
            part_copy(chunk, k).wait_recv()
            total = total + part_recv[k, at]
        mine[at] = total.astype(BF16)

    def halo_copy(d, neighbour, slot, s):
        return remote(
            chosen.at[d, s],
            near.at[slot, s, piece(pole)],
            halo_send_sem.at[d, s],
            halo_recv_sem.at[slot, s],
            {"sep": neighbour},
        )

    for s in range(slots):
        for d, there, neighbour in sides:

            @pl.when(there)
            def _():
                local = jnp.clip(list_smem[d, 0, s] - me * nblocks, 0, nblocks - 1)
                chosen[d, s] = mine[local]
                halo_copy(d, neighbour, 1 - d, s).start()

    def own_copy(k, q):
        return remote(
            mine, own.at[:, piece(q)], own_send_sem.at[k], own_recv_sem.at[k], {"pole": peer(k)}
        )

    for k in peers:
        own_copy(k, pole).start()
    own[:, piece(pole), :] = mine[...]

    ends = body_diag[...]
    for k in peers:
        pdiag_copy(k).wait_recv()
        ends = ends + part_diag[k]
    near_diag[1] = ends

    def hdiag_copy(d, neighbour, slot):
        return remote(
            near_diag.at[1],
            near_diag.at[2 * slot],
            hdiag_send_sem.at[d],
            hdiag_recv_sem.at[slot],
            {"sep": neighbour},
        )

    for d, there, neighbour in sides:

        @pl.when(there)
        def _():
            hdiag_copy(d, neighbour, 1 - d).start()

    loads[3].wait()
    for k in peers:
        own_copy(k, peer(n_pole - k)).wait_recv()
    for d, there, neighbour in sides:

        @pl.when(there)
        def _():
            hdiag_copy(d, neighbour, d).wait_recv()

    def fwd_copy(d, s, k, q):
        return remote(
            near.at[d, s, piece(pole)],
            near.at[d, s, piece(q)],
            fwd_send_sem.at[d, s, k],
            fwd_recv_sem.at[d, s, k],
            {"pole": peer(k)},
        )

    def forward(s):
        for d, there, neighbour in sides:

            @pl.when(there)
            def _():
                halo_copy(d, neighbour, d, s).wait_recv()
                for k in peers:
                    fwd_copy(d, s, k, pole).start()

    def contribution(s):
        for d, there, _ in sides:

            @pl.when(there)
            def _():
                for k in peers:
                    fwd_copy(d, s, k, peer(n_pole - k)).wait_recv()

        local = blocks_ref[0, s] - me * nblocks
        inside = jnp.clip(local, 0, nblocks - 1)
        block = jnp.where(local < 0, near[0, s], jnp.where(local < nblocks, own[inside], near[1, s]))
        before, here, after = (near_diag[i, pl.ds(j, 1), :] for i, j in (
            (0, jnp.clip(local + nblocks, 0, nblocks - 1)),
            (1, inside),
            (2, jnp.clip(local - nblocks, 0, nblocks - 1)),
        ))
        end = jnp.where(local < 0, before, jnp.where(local < nblocks, here, after))
        both = block[half:].astype(F32)
        first = jnp.where(below, 0.0, both).astype(BF16)
        second = jnp.where(below, both, 0.0).astype(BF16)
        matrix = jnp.concatenate(
            [
                jnp.concatenate([first, block[:half]], axis=1),
                jnp.concatenate([jnp.zeros_like(first), second], axis=1),
            ],
            axis=0,
        )
        value = values[s]
        inner = jnp.dot(value, matrix, preferred_element_type=F32)
        wide = value.astype(F32)
        left, right = wide[:, :half], wide[:, half:]
        each = left * inner[:, :half] + right * (inner[:, half:] + right * end)
        return jnp.where(s < count_ref[0], each, 0.0)

    total = jnp.zeros((values.shape[1], half), F32)
    forward(0)
    for s in range(slots):
        if s + 1 < slots:
            forward(s + 1)
        total = total + contribution(s)
    out_ref[...] = jnp.sum(total.T, axis=0, keepdims=True)

    for level in range(LEVELS):
        for copy in upper_copies(level):
            copy.wait_send()
    for k in peers:
        for chunk in range(CHUNKS):
            part_copy(chunk, k).wait_send()
        pdiag_copy(k).wait_send()
        own_copy(k, pole).wait_send()
    for d, there, neighbour in sides:

        @pl.when(there)
        def _():
            list_copy(d, neighbour, 1 - d).wait_send()
            hdiag_copy(d, neighbour, 1 - d).wait_send()
            for s in range(slots):
                halo_copy(d, neighbour, 1 - d, s).wait_send()
                for k in peers:
                    fwd_copy(d, s, k, pole).wait_send()


def shards(
    n_pole,
    n_sep,
    diag_inverse,
    coupling,
    ancestor_inverse,
    pole_weight,
    ancestor_bit,
    tile_blocks,
    tile_count,
    orbital_values,
):
    nblocks, _, width, _ = diag_inverse.shape[1:]
    slots, points = orbital_values.shape[1:3]
    half = width // 2
    rows = width // n_pole
    dma = pltpu.SemaphoreType.DMA
    scratch = [
        pltpu.VMEM(diag_inverse.shape[1:], BF16),
        pltpu.VMEM(coupling.shape[1:], BF16),
        pltpu.VMEM(ancestor_inverse.shape[2:], BF16),
        pltpu.VMEM(orbital_values.shape[1:], BF16),
        pltpu.VMEM((5, half, half), BF16),
        pltpu.VMEM((LEVELS, 5, half, half), BF16),
        pltpu.VMEM((LEVELS, 2 * width, 2 * width), BF16),
        pltpu.VMEM((nblocks, width, half), F32),
        pltpu.VMEM((nblocks, half), F32),
        pltpu.VMEM((n_pole, nblocks, rows, half), F32),
        pltpu.VMEM((n_pole, nblocks, rows, half), F32),
        pltpu.VMEM((n_pole, nblocks, half), F32),
        pltpu.VMEM((nblocks, rows, half), BF16),
        pltpu.VMEM((nblocks, width, half), BF16),
        pltpu.VMEM((2, slots, width, half), BF16),
        pltpu.VMEM((3, nblocks, half), F32),
        pltpu.VMEM((2, slots, rows, half), BF16),
        pltpu.VMEM((8, 128), jnp.int32),
        pltpu.VMEM((2, 8, 128), jnp.int32),
        pltpu.SMEM((2, 8, 128), jnp.int32),
        dma((4,)),
        dma((2,)),
        dma((LEVELS, 2)),
        dma((LEVELS, 2)),
        dma((CHUNKS, n_pole)),
        dma((CHUNKS, n_pole)),
        dma((n_pole,)),
        dma((n_pole,)),
        dma((n_pole,)),
        dma((n_pole,)),
        dma((2, slots)),
        dma((2, slots)),
        dma((2,)),
        dma((2,)),
        dma((2, slots, n_pole)),
        dma((2, slots, n_pole)),
        dma((2,)),
        dma((2,)),
    ]
    smem = pl.BlockSpec(memory_space=pltpu.SMEM)
    anywhere = pl.BlockSpec(memory_space=pl.ANY)
    return pl.pallas_call(
        functools.partial(kernel, n_pole, n_sep),
        out_shape=jax.ShapeDtypeStruct((1, points), F32),
        in_specs=[smem] * 4 + [anywhere] * 4,
        out_specs=pl.BlockSpec(memory_space=pltpu.VMEM),
        scratch_shapes=scratch,
        compiler_params=pltpu.CompilerParams(
            collective_id=0, has_side_effects=True, vmem_limit_bytes=60 * 1024 * 1024
        ),
    )(
        pole_weight,
        ancestor_bit,
        tile_blocks,
        tile_count,
        diag_inverse,
        coupling,
        ancestor_inverse,
        orbital_values,
    )


def solution(mesh):
    placed = (
        P("pole", "sep", None, None, None),
        P("pole", "sep", None, None, None),
        P("pole", "sep", None, None, None),
        P("pole", None),
        P("sep"),
        P("sep", None),
        P("sep"),
        P("sep", None, "pole", None),
    )
    return jax.shard_map(
        functools.partial(shards, mesh.shape["pole"], mesh.shape["sep"]),
        mesh=mesh,
        in_specs=placed,
        out_specs=P("sep", "pole"),
        check_vma=False,
    )
```

```python
import functools

import jax
import jax.numpy as jnp
from jax import lax
from jax.experimental import pallas as pl
from jax.experimental.pallas import tpu as pltpu
from jax.sharding import PartitionSpec as P

LEVELS = 4
CHUNKS = 4
EARLY = 3
MESH = pl.DeviceIdType.MESH
F32 = jnp.float32
BF16 = jnp.bfloat16


def nt_dot(left, right):
    return lax.dot_general(left, right, (((1,), (1,)), ((), ())), preferred_element_type=F32)


def kernel(
    n_pole,
    n_sep,
    weight_ref,
    bit_ref,
    blocks_ref,
    count_ref,
    diag_hbm,
    link_hbm,
    upper_hbm,
    values_hbm,
    out_ref,
    diag,
    link,
    upper,
    values,
    packed,
    arrived,
    full,
    body,
    body_diag,
    early,
    early_recv,
    part_recv,
    part_diag,
    mine,
    own,
    near,
    near_diag,
    chosen,
    list_send,
    list_recv,
    list_smem,
    local_sem,
    list_sem,
    upper_send_sem,
    upper_recv_sem,
    early_send_sem,
    early_recv_sem,
    part_send_sem,
    part_recv_sem,
    pdiag_send_sem,
    pdiag_recv_sem,
    own_send_sem,
    own_recv_sem,
    halo_send_sem,
    halo_recv_sem,
    hdiag_send_sem,
    hdiag_recv_sem,
    fwd_send_sem,
    fwd_recv_sem,
    list_send_sem,
    list_recv_sem,
):
    pole = lax.axis_index("pole")
    me = lax.axis_index("sep")
    nblocks = link.shape[0]
    slots = values.shape[0]
    half = packed.shape[1]
    rows = mine.shape[1]
    per_chunk = nblocks // CHUNKS
    peers = range(1, n_pole)

    def peer(k):
        return lax.rem(pole + k, n_pole)

    def piece(q):
        return pl.ds(pl.multiple_of(q * rows, rows), rows)

    def partner(level):
        step = 2**level
        return me + step * (1 - 2 * lax.rem(me // step, 2))

    sides = ((0, me > 0, me - 1), (1, me < n_sep - 1, me + 1))

    def remote(src, dst, send, recv, where):
        return pltpu.make_async_remote_copy(
            src_ref=src, dst_ref=dst, send_sem=send, recv_sem=recv, device_id=where, device_id_type=MESH
        )

    loads = [
        pltpu.make_async_copy(src, dst, local_sem.at[i])
        for i, (src, dst) in enumerate(
            (
                (upper_hbm.at[0, 0], upper),
                (diag_hbm.at[0], diag),
                (link_hbm.at[0], link),
                (values_hbm.at[0], values),
            )
        )
    ]
    for load in loads:
        load.start()

    barrier = pltpu.get_barrier_semaphore()
    for k in peers:
        pl.semaphore_signal(barrier, inc=1, device_id={"pole": peer(k)}, device_id_type=MESH)
    for level in range(LEVELS):
        pl.semaphore_signal(barrier, inc=1, device_id={"sep": partner(level)}, device_id_type=MESH)
    for _, there, neighbour in sides:

        @pl.when(there)
        def _():
            pl.semaphore_signal(barrier, inc=1, device_id={"sep": neighbour}, device_id_type=MESH)

    row = lax.broadcasted_iota(jnp.int32, (half, half), 0)
    col = lax.broadcasted_iota(jnp.int32, (half, half), 1)
    above, below, on = row < col, row > col, row == col

    def diagonal(x):
        return jnp.sum(jnp.where(on, x, 0.0), axis=0, keepdims=True)

    wr, wi = weight_ref[0, 0], weight_ref[0, 1]

    lane = lax.broadcasted_iota(jnp.int32, list_send.shape, 1)
    listed = jnp.zeros(list_send.shape, jnp.int32)
    for s in range(slots):
        listed = jnp.where(lane == s, blocks_ref[0, s], listed)
    list_send[...] = listed

    loads[0].wait()
    doubled = []
    for part in range(2):
        g00 = upper[part, :half, :half].astype(F32)
        g01 = upper[part, :half, half:].astype(F32)
        g10 = upper[part, half:, :half].astype(F32)
        g11 = upper[part, half:, half:].astype(F32)
        doubled.append((g00 + g00.T, g01 + g10.T, g11 + g11.T))
    weighted = (
        [wr * a - wi * b for a, b in zip(*doubled)],
        [wr * b + wi * a for a, b in zip(*doubled)],
    )
    ends = []
    for part in range(2):
        s00, s01, s11 = weighted[part]
        packed[2 * part] = s01.astype(BF16)
        packed[2 * part + 1] = jnp.where(below, s11, s00).astype(BF16)
        ends.append(diagonal(s11))
    packed[4] = jnp.where(row == 0, ends[0], jnp.where(row == 1, ends[1], 0.0)).astype(BF16)

    pl.semaphore_wait(
        barrier, n_pole - 1 + LEVELS + (me > 0).astype(jnp.int32) + (me < n_sep - 1).astype(jnp.int32)
    )

    def upper_copies(level):
        where = {"sep": partner(level)}
        return (
            remote(
                packed.at[pl.ds(0, 4)],
                arrived.at[level, pl.ds(0, 4)],
                upper_send_sem.at[level, 0],
                upper_recv_sem.at[level, 0],
                where,
            ),
            remote(
                packed.at[4, pl.ds(0, 16)],
                arrived.at[level, 4, pl.ds(0, 16)],
                upper_send_sem.at[level, 1],
                upper_recv_sem.at[level, 1],
                where,
            ),
        )

    for level in reversed(range(LEVELS)):
        for copy in upper_copies(level):
            copy.start()

    def list_copy(d, neighbour, slot):
        return remote(
            list_send, list_recv.at[slot], list_send_sem.at[d], list_recv_sem.at[slot], {"sep": neighbour}
        )

    for d, there, neighbour in sides:

        @pl.when(there)
        def _():
            list_copy(d, neighbour, 1 - d).start()

    loads[1].wait()

    def fold(b, carry):
        def term(rows_at, cols_at):
            real = diag[b, 0, rows_at, cols_at].astype(F32)
            imag = diag[b, 1, rows_at, cols_at].astype(F32)
            return wr * imag + wi * real

        low, high = pl.ds(0, half), pl.ds(half, half)
        t00, t01, t10, t11 = term(low, low), term(low, high), term(high, low), term(high, high)
        body[b, :half, :] = t01 + t10.T
        body[b, half:, :] = jnp.where(above, t00 + t00.T, jnp.where(below, t11 + t11.T, t00))
        body_diag[pl.ds(b, 1), :] = diagonal(t11)
        return carry

    lax.fori_loop(0, nblocks, fold, 0, unroll=2)
    loads[2].wait()

    for d, there, neighbour in sides:

        @pl.when(there)
        def _():
            list_copy(d, neighbour, d).wait_recv()
            fetch = pltpu.make_async_copy(list_recv.at[d], list_smem.at[d], list_sem.at[d])
            fetch.start()
            fetch.wait()

        @pl.when(jnp.logical_not(there))
        def _():
            fetch = pltpu.make_async_copy(list_send, list_smem.at[d], list_sem.at[d])
            fetch.start()
            fetch.wait()

    for level in range(LEVELS):
        for copy in upper_copies(level):
            copy.wait_recv()
        ends = arrived[level, 4, :16, :].astype(F32)
        symmetric = []
        for part in range(2):
            u01 = arrived[level, 2 * part]
            both = arrived[level, 2 * part + 1].astype(F32)
            turned = both.T
            g00 = jnp.where(below, turned, both)
            g11 = jnp.where(below, both, jnp.where(above, turned, ends[part : part + 1, :]))
            u10 = u01.astype(F32).T.astype(BF16)
            symmetric.append(((g00.astype(BF16), u01), (u10, g11.astype(BF16))))
        for i in range(2):
            for j in range(2):
                real, imag = symmetric[0][i][j], symmetric[1][i][j]
                r, c = i * half, j * half
                full[level, r : r + half, c : c + half] = real
                full[level, r : r + half, 2 * half + c : 3 * half + c] = imag
                full[level, 2 * half + r : 3 * half + r, c : c + half] = -imag
                full[level, 2 * half + r : 3 * half + r, 2 * half + c : 3 * half + c] = real

    def density(b):
        real, imag = link[b, 0], link[b, 1]
        middle = jnp.dot(
            jnp.concatenate([real, imag], axis=1), full[bit_ref[b]], preferred_element_type=F32
        ).astype(BF16)
        crossed = jnp.concatenate([imag, real], axis=1)
        top = nt_dot(middle[:half], crossed)
        low = nt_dot(middle[half:], crossed[half:])
        corner = top[:, :half]
        upper_right = body[b, :half, :] + top[:, half:]
        corners = body[b, half:, :] + jnp.where(above, corner, jnp.where(below, low, 0.5 * corner))
        return upper_right, corners, low

    def local_of(d, s):
        return jnp.clip(list_smem[d, 0, s] - me * nblocks, 0, nblocks - 1)

    def early_copy(s, k):
        return remote(
            early.at[s, :, piece(peer(k))],
            early_recv.at[k, s],
            early_send_sem.at[s, k],
            early_recv_sem.at[s, k],
            {"pole": peer(k)},
        )

    def part_copy(chunk, k):
        at = pl.ds(chunk * per_chunk, per_chunk)
        return remote(
            body.at[at, piece(peer(k))],
            part_recv.at[k, at],
            part_send_sem.at[chunk, k],
            part_recv_sem.at[chunk, k],
            {"pole": peer(k)},
        )

    def pdiag_copy(k):
        return remote(
            body_diag, part_diag.at[k], pdiag_send_sem.at[k], pdiag_recv_sem.at[k], {"pole": peer(k)}
        )

    def halo_copy(d, neighbour, slot, s):
        return remote(
            chosen.at[d, s],
            near.at[slot, s, piece(pole)],
            halo_send_sem.at[d, s],
            halo_recv_sem.at[slot, s],
            {"sep": neighbour},
        )

    def send_halo(s):
        for d, there, neighbour in sides:

            @pl.when(there)
            def _():
                halo_copy(d, neighbour, 1 - d, s).start()

    def finish_early(s):
        total = early[s, :, piece(pole), :]
        for k in peers:
            early_copy(s, k).wait_recv()
            total = total + early_recv[k, s]
        for d in range(2):
            chosen[d, s] = total[d].astype(BF16)
        send_halo(s)

    def finish_part(chunk):
        at = pl.ds(chunk * per_chunk, per_chunk)
        total = body[at, piece(pole), :]
        for k in peers:
            part_copy(chunk, k).wait_recv()
            total = total + part_recv[k, at]
        mine[at] = total.astype(BF16)

    for s in range(EARLY):
        for d in range(2):
            upper_right, corners, _ = density(local_of(d, s))
            early[s, d, :half, :] = upper_right
            early[s, d, half:, :] = corners
        for k in peers:
            early_copy(s, k).start()
        if s > 0:
            finish_early(s - 1)

    for chunk in range(CHUNKS):
        for b in range(chunk * per_chunk, (chunk + 1) * per_chunk):
            upper_right, corners, low = density(b)
            body[b, :half, :] = upper_right
            body[b, half:, :] = corners
            body_diag[b : b + 1, :] += 0.5 * diagonal(low)
        for k in peers:
            part_copy(chunk, k).start()
        if chunk == 0:
            finish_early(EARLY - 1)
        else:
            finish_part(chunk - 1)
    for k in peers:
        pdiag_copy(k).start()
    finish_part(CHUNKS - 1)

    for s in range(EARLY, slots):
        for d in range(2):
            chosen[d, s] = mine[local_of(d, s)]
        send_halo(s)

    def own_copy(k, q):
        return remote(
            mine, own.at[:, piece(q)], own_send_sem.at[k], own_recv_sem.at[k], {"pole": peer(k)}
        )

    for k in peers:
        own_copy(k, pole).start()
    own[:, piece(pole), :] = mine[...]

    ends = body_diag[...]
    for k in peers:
        pdiag_copy(k).wait_recv()
        ends = ends + part_diag[k]
    near_diag[1] = ends

    def hdiag_copy(d, neighbour, slot):
        return remote(
            near_diag.at[1],
            near_diag.at[2 * slot],
            hdiag_send_sem.at[d],
            hdiag_recv_sem.at[slot],
            {"sep": neighbour},
        )

    for d, there, neighbour in sides:

        @pl.when(there)
        def _():
            hdiag_copy(d, neighbour, 1 - d).start()

    loads[3].wait()
    for k in peers:
        own_copy(k, peer(n_pole - k)).wait_recv()

    def fwd_copy(d, s, k, q):
        return remote(
            near.at[d, s, piece(pole)],
            near.at[d, s, piece(q)],
            fwd_send_sem.at[d, s, k],
            fwd_recv_sem.at[d, s, k],
            {"pole": peer(k)},
        )

    def forward(s):
        for d, there, neighbour in sides:

            @pl.when(there)
            def _():
                halo_copy(d, neighbour, d, s).wait_recv()
                for k in peers:
                    fwd_copy(d, s, k, pole).start()

    def contribution(s):
        for d, there, _ in sides:

            @pl.when(there)
            def _():
                for k in peers:
                    fwd_copy(d, s, k, peer(n_pole - k)).wait_recv()

        local = blocks_ref[0, s] - me * nblocks
        inside = jnp.clip(local, 0, nblocks - 1)
        block = jnp.where(local < 0, near[0, s], jnp.where(local < nblocks, own[inside], near[1, s]))
        both = block[half:].astype(F32)
        first = jnp.where(below, 0.0, both).astype(BF16)
        second = jnp.where(below, both, 0.0).astype(BF16)
        matrix = jnp.concatenate(
            [
                jnp.concatenate([first, block[:half]], axis=1),
                jnp.concatenate([jnp.zeros_like(first), second], axis=1),
            ],
            axis=0,
        )
        value = values[s]
        inner = jnp.dot(value, matrix, preferred_element_type=F32)
        wide = value.astype(F32)
        left, right = wide[:, :half], wide[:, half:]
        each = left * inner[:, :half] + right * inner[:, half:]
        return jnp.where(s < count_ref[0], each, 0.0)

    def end_contribution(s):
        local = blocks_ref[0, s] - me * nblocks
        before, here, after = (
            near_diag[i, pl.ds(jnp.clip(local + (1 - i) * nblocks, 0, nblocks - 1), 1), :] for i in range(3)
        )
        end = jnp.where(local < 0, before, jnp.where(local < nblocks, here, after))
        right = values[s, :, half:].astype(F32)
        return jnp.where(s < count_ref[0], right * right * end, 0.0)

    total = jnp.zeros((values.shape[1], half), F32)
    forward(0)
    for s in range(slots):
        if s + 1 < slots:
            forward(s + 1)
        if s + 1 == slots:
            for d, there, neighbour in sides:

                @pl.when(there)
                def _():
                    hdiag_copy(d, neighbour, d).wait_recv()

            for i in range(slots):
                total = total + end_contribution(i)
        total = total + contribution(s)
    out_ref[...] = jnp.sum(total.T, axis=0, keepdims=True)

    for level in range(LEVELS):
        for copy in upper_copies(level):
            copy.wait_send()
    for k in peers:
        for s in range(EARLY):
            early_copy(s, k).wait_send()
        for chunk in range(CHUNKS):
            part_copy(chunk, k).wait_send()
        pdiag_copy(k).wait_send()
        own_copy(k, pole).wait_send()
    for d, there, neighbour in sides:

        @pl.when(there)
        def _():
            list_copy(d, neighbour, 1 - d).wait_send()
            hdiag_copy(d, neighbour, 1 - d).wait_send()
            for s in range(slots):
                halo_copy(d, neighbour, 1 - d, s).wait_send()
                for k in peers:
                    fwd_copy(d, s, k, pole).wait_send()


def shards(
    n_pole,
    n_sep,
    diag_inverse,
    coupling,
    ancestor_inverse,
    pole_weight,
    ancestor_bit,
    tile_blocks,
    tile_count,
    orbital_values,
):
    nblocks, _, width, _ = diag_inverse.shape[1:]
    slots, points = orbital_values.shape[1:3]
    half = width // 2
    rows = width // n_pole
    dma = pltpu.SemaphoreType.DMA
    scratch = [
        pltpu.VMEM(diag_inverse.shape[1:], BF16),
        pltpu.VMEM(coupling.shape[1:], BF16),
        pltpu.VMEM(ancestor_inverse.shape[2:], BF16),
        pltpu.VMEM(orbital_values.shape[1:], BF16),
        pltpu.VMEM((5, half, half), BF16),
        pltpu.VMEM((LEVELS, 5, half, half), BF16),
        pltpu.VMEM((LEVELS, 2 * width, 2 * width), BF16),
        pltpu.VMEM((nblocks, width, half), F32),
        pltpu.VMEM((nblocks, half), F32),
        pltpu.VMEM((EARLY, 2, width, half), F32),
        pltpu.VMEM((n_pole, EARLY, 2, rows, half), F32),
        pltpu.VMEM((n_pole, nblocks, rows, half), F32),
        pltpu.VMEM((n_pole, nblocks, half), F32),
        pltpu.VMEM((nblocks, rows, half), BF16),
        pltpu.VMEM((nblocks, width, half), BF16),
        pltpu.VMEM((2, slots, width, half), BF16),
        pltpu.VMEM((3, nblocks, half), F32),
        pltpu.VMEM((2, slots, rows, half), BF16),
        pltpu.VMEM((8, 128), jnp.int32),
        pltpu.VMEM((2, 8, 128), jnp.int32),
        pltpu.SMEM((2, 8, 128), jnp.int32),
        dma((4,)),
        dma((2,)),
        dma((LEVELS, 2)),
        dma((LEVELS, 2)),
        dma((EARLY, n_pole)),
        dma((EARLY, n_pole)),
        dma((CHUNKS, n_pole)),
        dma((CHUNKS, n_pole)),
        dma((n_pole,)),
        dma((n_pole,)),
        dma((n_pole,)),
        dma((n_pole,)),
        dma((2, slots)),
        dma((2, slots)),
        dma((2,)),
        dma((2,)),
        dma((2, slots, n_pole)),
        dma((2, slots, n_pole)),
        dma((2,)),
        dma((2,)),
    ]
    smem = pl.BlockSpec(memory_space=pltpu.SMEM)
    anywhere = pl.BlockSpec(memory_space=pl.ANY)
    return pl.pallas_call(
        functools.partial(kernel, n_pole, n_sep),
        out_shape=jax.ShapeDtypeStruct((1, points), F32),
        in_specs=[smem] * 4 + [anywhere] * 4,
        out_specs=pl.BlockSpec(memory_space=pltpu.VMEM),
        scratch_shapes=scratch,
        compiler_params=pltpu.CompilerParams(
            collective_id=0, has_side_effects=True, vmem_limit_bytes=60 * 1024 * 1024
        ),
    )(
        pole_weight,
        ancestor_bit,
        tile_blocks,
        tile_count,
        diag_inverse,
        coupling,
        ancestor_inverse,
        orbital_values,
    )


def solution(mesh):
    placed = (
        P("pole", "sep", None, None, None),
        P("pole", "sep", None, None, None),
        P("pole", "sep", None, None, None),
        P("pole", None),
        P("sep"),
        P("sep", None),
        P("sep"),
        P("sep", None, "pole", None),
    )
    return jax.shard_map(
        functools.partial(shards, mesh.shape["pole"], mesh.shape["sep"]),
        mesh=mesh,
        in_specs=placed,
        out_specs=P("sep", "pole"),
        check_vma=False,
    )
```

```python
import functools

import jax
import jax.numpy as jnp
from jax import lax
from jax.experimental import pallas as pl
from jax.experimental.pallas import tpu as pltpu
from jax.sharding import PartitionSpec as P

LEVELS = 4
CHUNKS = 4
EARLY = 4
MESH = pl.DeviceIdType.MESH
F32 = jnp.float32
BF16 = jnp.bfloat16


def nt_dot(left, right):
    return lax.dot_general(left, right, (((1,), (1,)), ((), ())), preferred_element_type=F32)


def kernel(
    n_pole,
    n_sep,
    weight_hbm,
    bit_hbm,
    blocks_hbm,
    count_ref,
    diag_hbm,
    link_hbm,
    upper_hbm,
    values_hbm,
    out_ref,
    weight_ref,
    bit_ref,
    blocks_ref,
    diag,
    link,
    upper,
    values,
    packed,
    arrived,
    full,
    body,
    body_diag,
    early,
    early_recv,
    part_recv,
    part_diag,
    mine,
    own,
    near,
    near_diag,
    chosen,
    list_send,
    list_recv,
    list_smem,
    local_sem,
    small_sem,
    list_sem,
    upper_send_sem,
    upper_recv_sem,
    early_send_sem,
    early_recv_sem,
    part_send_sem,
    part_recv_sem,
    pdiag_send_sem,
    pdiag_recv_sem,
    own_send_sem,
    own_recv_sem,
    halo_send_sem,
    halo_recv_sem,
    hdiag_send_sem,
    hdiag_recv_sem,
    fwd_send_sem,
    fwd_recv_sem,
    list_send_sem,
    list_recv_sem,
):
    pole = lax.axis_index("pole")
    me = lax.axis_index("sep")
    nblocks = link.shape[0]
    slots = values.shape[0]
    half = packed.shape[1]
    rows = mine.shape[1]
    per_chunk = nblocks // CHUNKS
    peers = range(1, n_pole)

    def peer(k):
        return lax.rem(pole + k, n_pole)

    def piece(q):
        return pl.ds(pl.multiple_of(q * rows, rows), rows)

    def partner(level):
        step = 2**level
        return me + step * (1 - 2 * lax.rem(me // step, 2))

    sides = ((0, me > 0, me - 1), (1, me < n_sep - 1, me + 1))

    def remote(src, dst, send, recv, where):
        return pltpu.make_async_remote_copy(
            src_ref=src, dst_ref=dst, send_sem=send, recv_sem=recv, device_id=where, device_id_type=MESH
        )

    loads = [
        pltpu.make_async_copy(src, dst, local_sem.at[i])
        for i, (src, dst) in enumerate(
            (
                (upper_hbm.at[0, 0], upper),
                (diag_hbm.at[0], diag),
                (link_hbm.at[0], link),
                (values_hbm.at[0], values),
            )
        )
    ]
    small = [
        pltpu.make_async_copy(src, dst, small_sem.at[i])
        for i, (src, dst) in enumerate(
            ((weight_hbm, weight_ref), (blocks_hbm, blocks_ref), (bit_hbm, bit_ref))
        )
    ]
    loads[0].start()
    for copy in small:
        copy.start()

    barrier = pltpu.get_barrier_semaphore()
    for k in peers:
        pl.semaphore_signal(barrier, inc=1, device_id={"pole": peer(k)}, device_id_type=MESH)
    for level in range(LEVELS):
        pl.semaphore_signal(barrier, inc=1, device_id={"sep": partner(level)}, device_id_type=MESH)
    for _, there, neighbour in sides:

        @pl.when(there)
        def _():
            pl.semaphore_signal(barrier, inc=1, device_id={"sep": neighbour}, device_id_type=MESH)

    row = lax.broadcasted_iota(jnp.int32, (half, half), 0)
    col = lax.broadcasted_iota(jnp.int32, (half, half), 1)
    above, below, on = row < col, row > col, row == col

    def diagonal(x):
        return jnp.sum(jnp.where(on, x, 0.0), axis=0, keepdims=True)

    for copy in small:
        copy.wait()
    wr, wi = weight_ref[0, 0], weight_ref[0, 1]

    lane = lax.broadcasted_iota(jnp.int32, list_send.shape, 1)
    listed = jnp.zeros(list_send.shape, jnp.int32)
    for s in range(slots):
        listed = jnp.where(lane == s, blocks_ref[0, s], listed)
    list_send[...] = listed

    loads[0].wait()
    for load in loads[1:]:
        load.start()
    doubled = []
    for part in range(2):
        g00 = upper[part, :half, :half].astype(F32)
        g01 = upper[part, :half, half:].astype(F32)
        g10 = upper[part, half:, :half].astype(F32)
        g11 = upper[part, half:, half:].astype(F32)
        doubled.append((g00 + g00.T, g01 + g10.T, g11 + g11.T))
    weighted = (
        [wr * a - wi * b for a, b in zip(*doubled)],
        [wr * b + wi * a for a, b in zip(*doubled)],
    )
    ends = []
    for part in range(2):
        s00, s01, s11 = weighted[part]
        packed[2 * part] = s01.astype(BF16)
        packed[2 * part + 1] = jnp.where(below, s11, s00).astype(BF16)
        ends.append(diagonal(s11))
    packed[4] = jnp.where(row == 0, ends[0], jnp.where(row == 1, ends[1], 0.0)).astype(BF16)

    pl.semaphore_wait(
        barrier, n_pole - 1 + LEVELS + (me > 0).astype(jnp.int32) + (me < n_sep - 1).astype(jnp.int32)
    )

    def upper_copies(level):
        where = {"sep": partner(level)}
        return (
            remote(
                packed.at[pl.ds(0, 4)],
                arrived.at[level, pl.ds(0, 4)],
                upper_send_sem.at[level, 0],
                upper_recv_sem.at[level, 0],
                where,
            ),
            remote(
                packed.at[4, pl.ds(0, 16)],
                arrived.at[level, 4, pl.ds(0, 16)],
                upper_send_sem.at[level, 1],
                upper_recv_sem.at[level, 1],
                where,
            ),
        )

    for level in reversed(range(LEVELS)):
        for copy in upper_copies(level):
            copy.start()

    def list_copy(d, neighbour, slot):
        return remote(
            list_send, list_recv.at[slot], list_send_sem.at[d], list_recv_sem.at[slot], {"sep": neighbour}
        )

    for d, there, neighbour in sides:

        @pl.when(there)
        def _():
            list_copy(d, neighbour, 1 - d).start()

    loads[1].wait()

    def fold(b, carry):
        def term(rows_at, cols_at):
            real = diag[b, 0, rows_at, cols_at].astype(F32)
            imag = diag[b, 1, rows_at, cols_at].astype(F32)
            return wr * imag + wi * real

        low, high = pl.ds(0, half), pl.ds(half, half)
        t00, t01, t10, t11 = term(low, low), term(low, high), term(high, low), term(high, high)
        body[b, :half, :] = t01 + t10.T
        body[b, half:, :] = jnp.where(above, t00 + t00.T, jnp.where(below, t11 + t11.T, t00))
        body_diag[pl.ds(b, 1), :] = diagonal(t11)
        return carry

    lax.fori_loop(0, nblocks, fold, 0, unroll=2)
    loads[2].wait()

    for d, there, neighbour in sides:

        @pl.when(there)
        def _():
            list_copy(d, neighbour, d).wait_recv()
            fetch = pltpu.make_async_copy(list_recv.at[d], list_smem.at[d], list_sem.at[d])
            fetch.start()
            fetch.wait()

        @pl.when(jnp.logical_not(there))
        def _():
            fetch = pltpu.make_async_copy(list_send, list_smem.at[d], list_sem.at[d])
            fetch.start()
            fetch.wait()

    for level in range(LEVELS):
        for copy in upper_copies(level):
            copy.wait_recv()
        ends = arrived[level, 4, :16, :].astype(F32)
        symmetric = []
        for part in range(2):
            u01 = arrived[level, 2 * part]
            both = arrived[level, 2 * part + 1].astype(F32)
            turned = both.T
            g00 = jnp.where(below, turned, both)
            g11 = jnp.where(below, both, jnp.where(above, turned, ends[part : part + 1, :]))
            u10 = u01.astype(F32).T.astype(BF16)
            symmetric.append(((g00.astype(BF16), u01), (u10, g11.astype(BF16))))
        for i in range(2):
            for j in range(2):
                real, imag = symmetric[0][i][j], symmetric[1][i][j]
                r, c = i * half, j * half
                full[level, r : r + half, c : c + half] = real
                full[level, r : r + half, 2 * half + c : 3 * half + c] = imag
                full[level, 2 * half + r : 3 * half + r, c : c + half] = -imag
                full[level, 2 * half + r : 3 * half + r, 2 * half + c : 3 * half + c] = real

    def density(b):
        real, imag = link[b, 0], link[b, 1]
        middle = jnp.dot(
            jnp.concatenate([real, imag], axis=1), full[bit_ref[b]], preferred_element_type=F32
        ).astype(BF16)
        crossed = jnp.concatenate([imag, real], axis=1)
        product = nt_dot(middle, crossed)
        corner, low = product[:half, :half], product[half:, half:]
        upper_right = body[b, :half, :] + product[:half, half:]
        corners = body[b, half:, :] + jnp.where(above, corner, jnp.where(below, low, 0.5 * corner))
        return upper_right, corners, low

    def local_of(d, s):
        return jnp.clip(list_smem[d, 0, s] - me * nblocks, 0, nblocks - 1)

    def early_copy(s, k):
        return remote(
            early.at[s, :, piece(peer(k))],
            early_recv.at[k, s],
            early_send_sem.at[s, k],
            early_recv_sem.at[s, k],
            {"pole": peer(k)},
        )

    def part_copy(chunk, k):
        at = pl.ds(chunk * per_chunk, per_chunk)
        return remote(
            body.at[at, piece(peer(k))],
            part_recv.at[k, at],
            part_send_sem.at[chunk, k],
            part_recv_sem.at[chunk, k],
            {"pole": peer(k)},
        )

    def pdiag_copy(k):
        return remote(
            body_diag, part_diag.at[k], pdiag_send_sem.at[k], pdiag_recv_sem.at[k], {"pole": peer(k)}
        )

    def halo_copy(d, neighbour, slot, s):
        return remote(
            chosen.at[d, s],
            near.at[slot, s, piece(pole)],
            halo_send_sem.at[d, s],
            halo_recv_sem.at[slot, s],
            {"sep": neighbour},
        )

    def send_halo(s):
        for d, there, neighbour in sides:

            @pl.when(there)
            def _():
                halo_copy(d, neighbour, 1 - d, s).start()

    def finish_early(s):
        total = early[s, :, piece(pole), :]
        for k in peers:
            early_copy(s, k).wait_recv()
            total = total + early_recv[k, s]
        for d in range(2):
            chosen[d, s] = total[d].astype(BF16)
        send_halo(s)

    def finish_part(chunk):
        at = pl.ds(chunk * per_chunk, per_chunk)
        total = body[at, piece(pole), :]
        for k in peers:
            part_copy(chunk, k).wait_recv()
            total = total + part_recv[k, at]
        mine[at] = total.astype(BF16)

    for s in range(EARLY):
        for d in range(2):
            upper_right, corners, _ = density(local_of(d, s))
            early[s, d, :half, :] = upper_right
            early[s, d, half:, :] = corners
        for k in peers:
            early_copy(s, k).start()
        if s > 0:
            finish_early(s - 1)

    for chunk in range(CHUNKS):
        for b in range(chunk * per_chunk, (chunk + 1) * per_chunk):
            upper_right, corners, low = density(b)
            body[b, :half, :] = upper_right
            body[b, half:, :] = corners
            body_diag[b : b + 1, :] += 0.5 * diagonal(low)
        for k in peers:
            part_copy(chunk, k).start()
        if chunk == 0:
            finish_early(EARLY - 1)
        else:
            finish_part(chunk - 1)
    for k in peers:
        pdiag_copy(k).start()
    finish_part(CHUNKS - 1)

    for s in range(EARLY, slots):
        for d in range(2):
            chosen[d, s] = mine[local_of(d, s)]
        send_halo(s)

    def own_copy(k, q):
        return remote(
            mine, own.at[:, piece(q)], own_send_sem.at[k], own_recv_sem.at[k], {"pole": peer(k)}
        )

    for k in peers:
        own_copy(k, pole).start()
    own[:, piece(pole), :] = mine[...]

    ends = body_diag[...]
    for k in peers:
        pdiag_copy(k).wait_recv()
        ends = ends + part_diag[k]
    near_diag[1] = ends

    def hdiag_copy(d, neighbour, slot):
        return remote(
            near_diag.at[1],
            near_diag.at[2 * slot],
            hdiag_send_sem.at[d],
            hdiag_recv_sem.at[slot],
            {"sep": neighbour},
        )

    for d, there, neighbour in sides:

        @pl.when(there)
        def _():
            hdiag_copy(d, neighbour, 1 - d).start()

    loads[3].wait()
    for k in peers:
        own_copy(k, peer(n_pole - k)).wait_recv()

    def fwd_copy(d, s, k, q):
        return remote(
            near.at[d, s, piece(pole)],
            near.at[d, s, piece(q)],
            fwd_send_sem.at[d, s, k],
            fwd_recv_sem.at[d, s, k],
            {"pole": peer(k)},
        )

    def forward(s):
        for d, there, neighbour in sides:

            @pl.when(there)
            def _():
                halo_copy(d, neighbour, d, s).wait_recv()
                for k in peers:
                    fwd_copy(d, s, k, pole).start()

    def contribution(s):
        for d, there, _ in sides:

            @pl.when(there)
            def _():
                for k in peers:
                    fwd_copy(d, s, k, peer(n_pole - k)).wait_recv()

        local = blocks_ref[0, s] - me * nblocks
        inside = jnp.clip(local, 0, nblocks - 1)
        block = jnp.where(local < 0, near[0, s], jnp.where(local < nblocks, own[inside], near[1, s]))
        both = block[half:].astype(F32)
        first = jnp.where(below, 0.0, both).astype(BF16)
        second = jnp.where(below, both, 0.0).astype(BF16)
        matrix = jnp.concatenate(
            [
                jnp.concatenate([first, block[:half]], axis=1),
                jnp.concatenate([jnp.zeros_like(first), second], axis=1),
            ],
            axis=0,
        )
        value = values[s]
        inner = jnp.dot(value, matrix, preferred_element_type=F32)
        wide = value.astype(F32)
        left, right = wide[:, :half], wide[:, half:]
        each = left * inner[:, :half] + right * inner[:, half:]
        return jnp.where(s < count_ref[0], each, 0.0)

    def end_contribution(s):
        local = blocks_ref[0, s] - me * nblocks
        before, here, after = (
            near_diag[i, pl.ds(jnp.clip(local + (1 - i) * nblocks, 0, nblocks - 1), 1), :] for i in range(3)
        )
        end = jnp.where(local < 0, before, jnp.where(local < nblocks, here, after))
        right = values[s, :, half:].astype(F32)
        return jnp.where(s < count_ref[0], right * right * end, 0.0)

    total = jnp.zeros((values.shape[1], half), F32)
    forward(0)
    for s in range(slots):
        if s + 1 < slots:
            forward(s + 1)
        if s + 1 == slots:
            for d, there, neighbour in sides:

                @pl.when(there)
                def _():
                    hdiag_copy(d, neighbour, d).wait_recv()

            for i in range(slots):
                total = total + end_contribution(i)
        total = total + contribution(s)
    out_ref[...] = jnp.sum(total.T, axis=0, keepdims=True)

    for level in range(LEVELS):
        for copy in upper_copies(level):
            copy.wait_send()
    for k in peers:
        for s in range(EARLY):
            early_copy(s, k).wait_send()
        for chunk in range(CHUNKS):
            part_copy(chunk, k).wait_send()
        pdiag_copy(k).wait_send()
        own_copy(k, pole).wait_send()
    for d, there, neighbour in sides:

        @pl.when(there)
        def _():
            list_copy(d, neighbour, 1 - d).wait_send()
            hdiag_copy(d, neighbour, 1 - d).wait_send()
            for s in range(slots):
                halo_copy(d, neighbour, 1 - d, s).wait_send()
                for k in peers:
                    fwd_copy(d, s, k, pole).wait_send()


def shards(
    n_pole,
    n_sep,
    diag_inverse,
    coupling,
    ancestor_inverse,
    pole_weight,
    ancestor_bit,
    tile_blocks,
    tile_count,
    orbital_values,
):
    nblocks, _, width, _ = diag_inverse.shape[1:]
    slots, points = orbital_values.shape[1:3]
    half = width // 2
    rows = width // n_pole
    dma = pltpu.SemaphoreType.DMA
    scratch = [
        pltpu.SMEM(pole_weight.shape, F32),
        pltpu.SMEM(ancestor_bit.shape, jnp.int32),
        pltpu.SMEM(tile_blocks.shape, jnp.int32),
        pltpu.VMEM(diag_inverse.shape[1:], BF16),
        pltpu.VMEM(coupling.shape[1:], BF16),
        pltpu.VMEM(ancestor_inverse.shape[2:], BF16),
        pltpu.VMEM(orbital_values.shape[1:], BF16),
        pltpu.VMEM((5, half, half), BF16),
        pltpu.VMEM((LEVELS, 5, half, half), BF16),
        pltpu.VMEM((LEVELS, 2 * width, 2 * width), BF16),
        pltpu.VMEM((nblocks, width, half), F32),
        pltpu.VMEM((nblocks, half), F32),
        pltpu.VMEM((EARLY, 2, width, half), F32),
        pltpu.VMEM((n_pole, EARLY, 2, rows, half), F32),
        pltpu.VMEM((n_pole, nblocks, rows, half), F32),
        pltpu.VMEM((n_pole, nblocks, half), F32),
        pltpu.VMEM((nblocks, rows, half), BF16),
        pltpu.VMEM((nblocks, width, half), BF16),
        pltpu.VMEM((2, slots, width, half), BF16),
        pltpu.VMEM((3, nblocks, half), F32),
        pltpu.VMEM((2, slots, rows, half), BF16),
        pltpu.VMEM((8, 128), jnp.int32),
        pltpu.VMEM((2, 8, 128), jnp.int32),
        pltpu.SMEM((2, 8, 128), jnp.int32),
        dma((4,)),
        dma((3,)),
        dma((2,)),
        dma((LEVELS, 2)),
        dma((LEVELS, 2)),
        dma((EARLY, n_pole)),
        dma((EARLY, n_pole)),
        dma((CHUNKS, n_pole)),
        dma((CHUNKS, n_pole)),
        dma((n_pole,)),
        dma((n_pole,)),
        dma((n_pole,)),
        dma((n_pole,)),
        dma((2, slots)),
        dma((2, slots)),
        dma((2,)),
        dma((2,)),
        dma((2, slots, n_pole)),
        dma((2, slots, n_pole)),
        dma((2,)),
        dma((2,)),
    ]
    hbm = pl.BlockSpec(memory_space=pl.ANY)
    return pl.pallas_call(
        functools.partial(kernel, n_pole, n_sep),
        out_shape=jax.ShapeDtypeStruct((1, points), F32),
        in_specs=[hbm] * 3 + [pl.BlockSpec(memory_space=pltpu.SMEM)] + [hbm] * 4,
        out_specs=pl.BlockSpec(memory_space=pltpu.VMEM),
        scratch_shapes=scratch,
        compiler_params=pltpu.CompilerParams(
            collective_id=0, has_side_effects=True, vmem_limit_bytes=60 * 1024 * 1024
        ),
    )(
        pole_weight,
        ancestor_bit,
        tile_blocks,
        tile_count,
        diag_inverse,
        coupling,
        ancestor_inverse,
        orbital_values,
    )


def solution(mesh):
    placed = (
        P("pole", "sep", None, None, None),
        P("pole", "sep", None, None, None),
        P("pole", "sep", None, None, None),
        P("pole", None),
        P("sep"),
        P("sep", None),
        P("sep"),
        P("sep", None, "pole", None),
    )
    return jax.shard_map(
        functools.partial(shards, mesh.shape["pole"], mesh.shape["sep"]),
        mesh=mesh,
        in_specs=placed,
        out_specs=P("sep", "pole"),
        check_vma=False,
    )
```

```python
import functools

import jax
import jax.numpy as jnp
from jax import lax
from jax.experimental import pallas as pl
from jax.experimental.pallas import tpu as pltpu
from jax.sharding import PartitionSpec as P

LEVELS = 4
CHUNKS = 4
EARLY = 4
MESH = pl.DeviceIdType.MESH
F32 = jnp.float32
BF16 = jnp.bfloat16


def nt_dot(left, right):
    return lax.dot_general(left, right, (((1,), (1,)), ((), ())), preferred_element_type=F32)


def kernel(
    n_pole,
    n_sep,
    weight_hbm,
    bit_hbm,
    blocks_hbm,
    count_ref,
    diag_hbm,
    link_hbm,
    upper_hbm,
    values_hbm,
    out_ref,
    weight_ref,
    bit_ref,
    blocks_ref,
    diag,
    link,
    upper,
    values,
    packed,
    arrived,
    full,
    body,
    body_diag,
    early,
    early_recv,
    part_recv,
    part_diag,
    mine,
    own,
    near,
    near_diag,
    chosen,
    list_send,
    list_recv,
    list_smem,
    local_sem,
    small_sem,
    list_sem,
    upper_send_sem,
    upper_recv_sem,
    early_send_sem,
    early_recv_sem,
    part_send_sem,
    part_recv_sem,
    pdiag_send_sem,
    pdiag_recv_sem,
    own_send_sem,
    own_recv_sem,
    halo_send_sem,
    halo_recv_sem,
    hdiag_send_sem,
    hdiag_recv_sem,
    fwd_send_sem,
    fwd_recv_sem,
    list_send_sem,
    list_recv_sem,
):
    pole = lax.axis_index("pole")
    me = lax.axis_index("sep")
    nblocks = link.shape[0]
    slots = values.shape[0]
    half = packed.shape[1]
    rows = mine.shape[1]
    per_chunk = nblocks // CHUNKS
    peers = range(1, n_pole)

    def peer(k):
        return lax.rem(pole + k, n_pole)

    def piece(q):
        return pl.ds(pl.multiple_of(q * rows, rows), rows)

    def partner(level):
        step = 2**level
        return me + step * (1 - 2 * lax.rem(me // step, 2))

    sides = ((0, me > 0, me - 1), (1, me < n_sep - 1, me + 1))

    def remote(src, dst, send, recv, where):
        return pltpu.make_async_remote_copy(
            src_ref=src, dst_ref=dst, send_sem=send, recv_sem=recv, device_id=where, device_id_type=MESH
        )

    loads = [
        pltpu.make_async_copy(src, dst, local_sem.at[i])
        for i, (src, dst) in enumerate(
            (
                (upper_hbm.at[0, 0], upper),
                (diag_hbm.at[0], diag),
                (link_hbm.at[0], link),
                (values_hbm.at[0], values),
            )
        )
    ]
    small = [
        pltpu.make_async_copy(src, dst, small_sem.at[i])
        for i, (src, dst) in enumerate(
            ((weight_hbm, weight_ref), (blocks_hbm, blocks_ref), (bit_hbm, bit_ref))
        )
    ]
    loads[0].start()
    for copy in small:
        copy.start()

    barrier = pltpu.get_barrier_semaphore()
    for k in peers:
        pl.semaphore_signal(barrier, inc=1, device_id={"pole": peer(k)}, device_id_type=MESH)
    for level in range(LEVELS):
        pl.semaphore_signal(barrier, inc=1, device_id={"sep": partner(level)}, device_id_type=MESH)
    for _, there, neighbour in sides:

        @pl.when(there)
        def _():
            pl.semaphore_signal(barrier, inc=1, device_id={"sep": neighbour}, device_id_type=MESH)

    row = lax.broadcasted_iota(jnp.int32, (half, half), 0)
    col = lax.broadcasted_iota(jnp.int32, (half, half), 1)
    above, below, on = row < col, row > col, row == col

    def diagonal(x):
        return jnp.sum(jnp.where(on, x, 0.0), axis=0, keepdims=True)

    for copy in small:
        copy.wait()
    wr, wi = weight_ref[0, 0], weight_ref[0, 1]

    lane = lax.broadcasted_iota(jnp.int32, list_send.shape, 1)
    listed = jnp.zeros(list_send.shape, jnp.int32)
    for s in range(slots):
        listed = jnp.where(lane == s, blocks_ref[0, s], listed)
    list_send[...] = listed

    loads[0].wait()
    for load in loads[1:]:
        load.start()
    doubled = []
    for part in range(2):
        g00 = upper[part, :half, :half].astype(F32)
        g01 = upper[part, :half, half:].astype(F32)
        g10 = upper[part, half:, :half].astype(F32)
        g11 = upper[part, half:, half:].astype(F32)
        doubled.append((g00 + g00.T, g01 + g10.T, g11 + g11.T))
    weighted = (
        [wr * a - wi * b for a, b in zip(*doubled)],
        [wr * b + wi * a for a, b in zip(*doubled)],
    )
    ends = []
    for part in range(2):
        s00, s01, s11 = weighted[part]
        packed[2 * part] = s01.astype(BF16)
        packed[2 * part + 1] = jnp.where(below, s11, s00).astype(BF16)
        ends.append(diagonal(s11))
    packed[4] = jnp.where(row == 0, ends[0], jnp.where(row == 1, ends[1], 0.0)).astype(BF16)

    pl.semaphore_wait(
        barrier, n_pole - 1 + LEVELS + (me > 0).astype(jnp.int32) + (me < n_sep - 1).astype(jnp.int32)
    )

    def upper_copies(level):
        where = {"sep": partner(level)}
        return (
            remote(
                packed.at[pl.ds(0, 4)],
                arrived.at[level, pl.ds(0, 4)],
                upper_send_sem.at[level, 0],
                upper_recv_sem.at[level, 0],
                where,
            ),
            remote(
                packed.at[4, pl.ds(0, 16)],
                arrived.at[level, 4, pl.ds(0, 16)],
                upper_send_sem.at[level, 1],
                upper_recv_sem.at[level, 1],
                where,
            ),
        )

    for level in reversed(range(LEVELS)):
        for copy in upper_copies(level):
            copy.start()

    def list_copy(d, neighbour, slot):
        return remote(
            list_send, list_recv.at[slot], list_send_sem.at[d], list_recv_sem.at[slot], {"sep": neighbour}
        )

    for d, there, neighbour in sides:

        @pl.when(there)
        def _():
            list_copy(d, neighbour, 1 - d).start()

    loads[1].wait()

    def fold(pair, carry):
        def folded(b):
            def term(rows_at, cols_at):
                real = diag[b, 0, rows_at, cols_at].astype(F32)
                imag = diag[b, 1, rows_at, cols_at].astype(F32)
                return wr * imag + wi * real

            low, high = pl.ds(0, half), pl.ds(half, half)
            t00, t01, t10, t11 = term(low, low), term(low, high), term(high, low), term(high, high)
            corners = jnp.where(above, t00 + t00.T, jnp.where(below, t11 + t11.T, t00))
            return t01 + t10.T, corners, diagonal(t11)

        at = [2 * pair, 2 * pair + 1]
        for b, (upper_right, corners, end) in zip(at, [folded(b) for b in at]):
            body[b, :half, :] = upper_right
            body[b, half:, :] = corners
            body_diag[pl.ds(b, 1), :] = end
        return carry

    lax.fori_loop(0, nblocks // 2, fold, 0)
    loads[2].wait()

    for d, there, neighbour in sides:

        @pl.when(there)
        def _():
            list_copy(d, neighbour, d).wait_recv()
            fetch = pltpu.make_async_copy(list_recv.at[d], list_smem.at[d], list_sem.at[d])
            fetch.start()
            fetch.wait()

        @pl.when(jnp.logical_not(there))
        def _():
            fetch = pltpu.make_async_copy(list_send, list_smem.at[d], list_sem.at[d])
            fetch.start()
            fetch.wait()

    for level in range(LEVELS):
        for copy in upper_copies(level):
            copy.wait_recv()
        ends = arrived[level, 4, :16, :].astype(F32)
        symmetric = []
        for part in range(2):
            u01 = arrived[level, 2 * part]
            both = arrived[level, 2 * part + 1].astype(F32)
            turned = both.T
            g00 = jnp.where(below, turned, both)
            g11 = jnp.where(below, both, jnp.where(above, turned, ends[part : part + 1, :]))
            u10 = u01.astype(F32).T.astype(BF16)
            symmetric.append(((g00.astype(BF16), u01), (u10, g11.astype(BF16))))
        for i in range(2):
            for j in range(2):
                real, imag = symmetric[0][i][j], symmetric[1][i][j]
                r, c = i * half, j * half
                full[level, r : r + half, c : c + half] = real
                full[level, r : r + half, 2 * half + c : 3 * half + c] = imag
                full[level, 2 * half + r : 3 * half + r, c : c + half] = -imag
                full[level, 2 * half + r : 3 * half + r, 2 * half + c : 3 * half + c] = real

    def middle_of(b):
        both = jnp.concatenate([link[b, 0], link[b, 1]], axis=1)
        return jnp.dot(both, full[bit_ref[b]], preferred_element_type=F32).astype(BF16)

    def density(b, middle):
        product = nt_dot(middle, jnp.concatenate([link[b, 1], link[b, 0]], axis=1))
        corner, low = product[:half, :half], product[half:, half:]
        upper_right = body[b, :half, :] + product[:half, half:]
        corners = body[b, half:, :] + jnp.where(above, corner, jnp.where(below, low, 0.5 * corner))
        return upper_right, corners, low

    def local_of(d, s):
        return jnp.clip(list_smem[d, 0, s] - me * nblocks, 0, nblocks - 1)

    def early_copy(s, k):
        return remote(
            early.at[s, :, piece(peer(k))],
            early_recv.at[k, s],
            early_send_sem.at[s, k],
            early_recv_sem.at[s, k],
            {"pole": peer(k)},
        )

    def part_copy(chunk, k):
        at = pl.ds(chunk * per_chunk, per_chunk)
        return remote(
            body.at[at, piece(peer(k))],
            part_recv.at[k, at],
            part_send_sem.at[chunk, k],
            part_recv_sem.at[chunk, k],
            {"pole": peer(k)},
        )

    def pdiag_copy(k):
        return remote(
            body_diag, part_diag.at[k], pdiag_send_sem.at[k], pdiag_recv_sem.at[k], {"pole": peer(k)}
        )

    def halo_copy(d, neighbour, slot, s):
        return remote(
            chosen.at[d, s],
            near.at[slot, s, piece(pole)],
            halo_send_sem.at[d, s],
            halo_recv_sem.at[slot, s],
            {"sep": neighbour},
        )

    def send_halo(s):
        for d, there, neighbour in sides:

            @pl.when(there)
            def _():
                halo_copy(d, neighbour, 1 - d, s).start()

    def finish_early(s):
        total = early[s, :, piece(pole), :]
        for k in peers:
            early_copy(s, k).wait_recv()
            total = total + early_recv[k, s]
        for d in range(2):
            chosen[d, s] = total[d].astype(BF16)
        send_halo(s)

    def finish_part(chunk):
        at = pl.ds(chunk * per_chunk, per_chunk)
        total = body[at, piece(pole), :]
        for k in peers:
            part_copy(chunk, k).wait_recv()
            total = total + part_recv[k, at]
        mine[at] = total.astype(BF16)

    groups = [[local_of(d, s) for d in range(2)] for s in range(EARLY)]
    groups += [list(range(c * per_chunk, (c + 1) * per_chunk)) for c in range(CHUNKS)]
    following = [middle_of(b) for b in groups[0]]
    for g, group in enumerate(groups):
        middles = following
        following = [middle_of(b) for b in groups[g + 1]] if g + 1 < len(groups) else []
        results = [density(b, middle) for b, middle in zip(group, middles)]
        if g < EARLY:
            for d, (upper_right, corners, _) in enumerate(results):
                early[g, d, :half, :] = upper_right
                early[g, d, half:, :] = corners
            for k in peers:
                early_copy(g, k).start()
        else:
            for b, (upper_right, corners, low) in zip(group, results):
                body[b, :half, :] = upper_right
                body[b, half:, :] = corners
                body_diag[b : b + 1, :] += 0.5 * diagonal(low)
            for k in peers:
                part_copy(g - EARLY, k).start()
        if 1 <= g <= EARLY:
            finish_early(g - 1)
        elif g > EARLY:
            finish_part(g - EARLY - 1)
    for k in peers:
        pdiag_copy(k).start()
    finish_part(CHUNKS - 1)

    for s in range(EARLY, slots):
        for d in range(2):
            chosen[d, s] = mine[local_of(d, s)]
        send_halo(s)

    def own_copy(k, q):
        return remote(
            mine, own.at[:, piece(q)], own_send_sem.at[k], own_recv_sem.at[k], {"pole": peer(k)}
        )

    for k in peers:
        own_copy(k, pole).start()
    own[:, piece(pole), :] = mine[...]

    ends = body_diag[...]
    for k in peers:
        pdiag_copy(k).wait_recv()
        ends = ends + part_diag[k]
    near_diag[1] = ends

    def hdiag_copy(d, neighbour, slot):
        return remote(
            near_diag.at[1],
            near_diag.at[2 * slot],
            hdiag_send_sem.at[d],
            hdiag_recv_sem.at[slot],
            {"sep": neighbour},
        )

    for d, there, neighbour in sides:

        @pl.when(there)
        def _():
            hdiag_copy(d, neighbour, 1 - d).start()

    loads[3].wait()
    for k in peers:
        own_copy(k, peer(n_pole - k)).wait_recv()

    def fwd_copy(d, s, k, q):
        return remote(
            near.at[d, s, piece(pole)],
            near.at[d, s, piece(q)],
            fwd_send_sem.at[d, s, k],
            fwd_recv_sem.at[d, s, k],
            {"pole": peer(k)},
        )

    def forward(s):
        for d, there, neighbour in sides:

            @pl.when(there)
            def _():
                halo_copy(d, neighbour, d, s).wait_recv()
                for k in peers:
                    fwd_copy(d, s, k, pole).start()

    def contribution(s):
        for d, there, _ in sides:

            @pl.when(there)
            def _():
                for k in peers:
                    fwd_copy(d, s, k, peer(n_pole - k)).wait_recv()

        local = blocks_ref[0, s] - me * nblocks
        inside = jnp.clip(local, 0, nblocks - 1)
        block = jnp.where(local < 0, near[0, s], jnp.where(local < nblocks, own[inside], near[1, s]))
        both = block[half:].astype(F32)
        first = jnp.where(below, 0.0, both).astype(BF16)
        second = jnp.where(below, both, 0.0).astype(BF16)
        matrix = jnp.concatenate(
            [
                jnp.concatenate([first, block[:half]], axis=1),
                jnp.concatenate([jnp.zeros_like(first), second], axis=1),
            ],
            axis=0,
        )
        value = values[s]
        inner = jnp.dot(value, matrix, preferred_element_type=F32)
        wide = value.astype(F32)
        left, right = wide[:, :half], wide[:, half:]
        each = left * inner[:, :half] + right * inner[:, half:]
        return jnp.where(s < count_ref[0], each, 0.0)

    def end_contribution(s):
        local = blocks_ref[0, s] - me * nblocks
        before, here, after = (
            near_diag[i, pl.ds(jnp.clip(local + (1 - i) * nblocks, 0, nblocks - 1), 1), :] for i in range(3)
        )
        end = jnp.where(local < 0, before, jnp.where(local < nblocks, here, after))
        right = values[s, :, half:].astype(F32)
        return jnp.where(s < count_ref[0], right * right * end, 0.0)

    total = jnp.zeros((values.shape[1], half), F32)
    forward(0)
    for s in range(slots):
        if s + 1 < slots:
            forward(s + 1)
        if s + 1 == slots:
            for d, there, neighbour in sides:

                @pl.when(there)
                def _():
                    hdiag_copy(d, neighbour, d).wait_recv()

            for i in range(slots):
                total = total + end_contribution(i)
        total = total + contribution(s)
    out_ref[...] = jnp.sum(total.T, axis=0, keepdims=True)

    for level in range(LEVELS):
        for copy in upper_copies(level):
            copy.wait_send()
    for k in peers:
        for s in range(EARLY):
            early_copy(s, k).wait_send()
        for chunk in range(CHUNKS):
            part_copy(chunk, k).wait_send()
        pdiag_copy(k).wait_send()
        own_copy(k, pole).wait_send()
    for d, there, neighbour in sides:

        @pl.when(there)
        def _():
            list_copy(d, neighbour, 1 - d).wait_send()
            hdiag_copy(d, neighbour, 1 - d).wait_send()
            for s in range(slots):
                halo_copy(d, neighbour, 1 - d, s).wait_send()
                for k in peers:
                    fwd_copy(d, s, k, pole).wait_send()


def shards(
    n_pole,
    n_sep,
    diag_inverse,
    coupling,
    ancestor_inverse,
    pole_weight,
    ancestor_bit,
    tile_blocks,
    tile_count,
    orbital_values,
):
    nblocks, _, width, _ = diag_inverse.shape[1:]
    slots, points = orbital_values.shape[1:3]
    half = width // 2
    rows = width // n_pole
    dma = pltpu.SemaphoreType.DMA
    scratch = [
        pltpu.SMEM(pole_weight.shape, F32),
        pltpu.SMEM(ancestor_bit.shape, jnp.int32),
        pltpu.SMEM(tile_blocks.shape, jnp.int32),
        pltpu.VMEM(diag_inverse.shape[1:], BF16),
        pltpu.VMEM(coupling.shape[1:], BF16),
        pltpu.VMEM(ancestor_inverse.shape[2:], BF16),
        pltpu.VMEM(orbital_values.shape[1:], BF16),
        pltpu.VMEM((5, half, half), BF16),
        pltpu.VMEM((LEVELS, 5, half, half), BF16),
        pltpu.VMEM((LEVELS, 2 * width, 2 * width), BF16),
        pltpu.VMEM((nblocks, width, half), F32),
        pltpu.VMEM((nblocks, half), F32),
        pltpu.VMEM((EARLY, 2, width, half), F32),
        pltpu.VMEM((n_pole, EARLY, 2, rows, half), F32),
        pltpu.VMEM((n_pole, nblocks, rows, half), F32),
        pltpu.VMEM((n_pole, nblocks, half), F32),
        pltpu.VMEM((nblocks, rows, half), BF16),
        pltpu.VMEM((nblocks, width, half), BF16),
        pltpu.VMEM((2, slots, width, half), BF16),
        pltpu.VMEM((3, nblocks, half), F32),
        pltpu.VMEM((2, slots, rows, half), BF16),
        pltpu.VMEM((8, 128), jnp.int32),
        pltpu.VMEM((2, 8, 128), jnp.int32),
        pltpu.SMEM((2, 8, 128), jnp.int32),
        dma((4,)),
        dma((3,)),
        dma((2,)),
        dma((LEVELS, 2)),
        dma((LEVELS, 2)),
        dma((EARLY, n_pole)),
        dma((EARLY, n_pole)),
        dma((CHUNKS, n_pole)),
        dma((CHUNKS, n_pole)),
        dma((n_pole,)),
        dma((n_pole,)),
        dma((n_pole,)),
        dma((n_pole,)),
        dma((2, slots)),
        dma((2, slots)),
        dma((2,)),
        dma((2,)),
        dma((2, slots, n_pole)),
        dma((2, slots, n_pole)),
        dma((2,)),
        dma((2,)),
    ]
    hbm = pl.BlockSpec(memory_space=pl.ANY)
    return pl.pallas_call(
        functools.partial(kernel, n_pole, n_sep),
        out_shape=jax.ShapeDtypeStruct((1, points), F32),
        in_specs=[hbm] * 3 + [pl.BlockSpec(memory_space=pltpu.SMEM)] + [hbm] * 4,
        out_specs=pl.BlockSpec(memory_space=pltpu.VMEM),
        scratch_shapes=scratch,
        compiler_params=pltpu.CompilerParams(
            collective_id=0, has_side_effects=True, vmem_limit_bytes=60 * 1024 * 1024
        ),
    )(
        pole_weight,
        ancestor_bit,
        tile_blocks,
        tile_count,
        diag_inverse,
        coupling,
        ancestor_inverse,
        orbital_values,
    )


def solution(mesh):
    placed = (
        P("pole", "sep", None, None, None),
        P("pole", "sep", None, None, None),
        P("pole", "sep", None, None, None),
        P("pole", None),
        P("sep"),
        P("sep", None),
        P("sep"),
        P("sep", None, "pole", None),
    )
    return jax.shard_map(
        functools.partial(shards, mesh.shape["pole"], mesh.shape["sep"]),
        mesh=mesh,
        in_specs=placed,
        out_specs=P("sep", "pole"),
        check_vma=False,
    )
```
